256 devices in a mesh: kx: 4 (over x), ky: 4 (over z_hi), kz: 16 (over z_lo, y, core).
Axes of the slice: x: 4, y: 4, z: 8 (z_hi: 4, z_lo: 2; z = z_hi * 2 + z_lo), core: 2. Of those that a mesh axis runs over, the one named last changes fastest.
Arguments:
- orbitals: bfloat16 [16, 16, 16, 1024, 128], P('kx', 'ky', 'kz'), may hold values from -6 to 6
- kernel: bfloat16 [256, 2, 1024, 1024], P(('kx', 'ky', 'kz')), may hold values from -0.00015258789 to 0.00015258789
- plan: int32 [2, 2, 256], replicated, may hold values from 0 to 15, as said below
- occupation: int32 [16, 16, 16, 64], replicated, may hold values 0 or 1
Outputs:
- exchange_blocks: float32 [16, 16, 16, 64, 128], P('kx', 'ky', 'kz')
The draws below stay inside these ranges and needn't reach their ends.
Inputs may be any that keep to these rules, and one draw needn't show every extreme that they name: `plan`: entry [r, 0, e] is the slot, in device e's block of 4 x 4 x 1 k-points, of the k-point that e sends as k in round r, and [r, 1, e] the slot of the one it sends as p. For every owner, k minus p is the same momentum transfer on the periodic k-mesh in every round.
All inputs are finite; a program needn't handle non-finite values.
Results may differ from the reference program's by a relative error of at most 0.004.
Values may be sent and summed in bfloat16 or wider, within the bound.
A program may use at most 128 MiB of HBM per device.

```python
import jax
import jax.numpy as jnp
from jax import lax

NMU = 1024
NB = 64
CX = 4
CY = 4
CZ = 1
ROUNDS = 2
MX = 16
MY = 16
MZ = 16
OWNERS = 256
N_KX = 4
N_KY = 4
N_KZ = 16


def hop_shifts_drawn(turn_number, mesh_counts):
    forward = ((turn_number + 1) % mesh_counts[0], (2 * turn_number + 1) % mesh_counts[1], (3 * turn_number + 1) % mesh_counts[2])
    partner = (forward[0], forward[1], (forward[2] - mesh_counts[2] // 2) % mesh_counts[2])
    return (forward, partner)


def sender_linear(owner_coords, shift, mesh_counts):
    sender_first = (owner_coords[0] - shift[0]) % mesh_counts[0]
    sender_second = (owner_coords[1] - shift[1]) % mesh_counts[1]
    sender_third = (owner_coords[2] - shift[2]) % mesh_counts[2]
    return (sender_first * mesh_counts[1] + sender_second) * mesh_counts[2] + sender_third


def draw_plan(key, part):
    mesh_counts = (N_KX, N_KY, N_KZ)
    cell_counts = (CX, CY, CZ)
    owner_total = N_KX * N_KY * N_KZ
    owners = jnp.arange(owner_total, dtype=jnp.int32)
    owner_coords = (owners // (N_KY * N_KZ), owners // N_KZ % N_KY, owners % N_KZ)
    offsets = []
    for dimension in range(3):
        offsets.append(jax.random.randint(jax.random.fold_in(key, 100 + dimension), (owner_total,), -(cell_counts[dimension] - 1), cell_counts[dimension]))
    rows_out = []
    for turn_number in range(ROUNDS):
        forward, partner = hop_shifts_drawn(turn_number, mesh_counts)
        first_cells = []
        second_cells = []
        for dimension in range(3):
            lowest = jnp.maximum(0, -offsets[dimension])
            highest = cell_counts[dimension] - jnp.maximum(0, offsets[dimension])
            chosen = jax.random.randint(jax.random.fold_in(key, 1000 * turn_number + dimension + 7), (owner_total,), lowest, highest)
            second_cells.append(chosen)
            first_cells.append(chosen + offsets[dimension])
        first_slot = (first_cells[0] * CY + first_cells[1]) * CZ + first_cells[2]
        second_slot = (second_cells[0] * CY + second_cells[1]) * CZ + second_cells[2]
        first_row = jnp.zeros((owner_total,), jnp.int32).at[sender_linear(owner_coords, forward, mesh_counts)].set(first_slot.astype(jnp.int32))
        second_row = jnp.zeros((owner_total,), jnp.int32).at[sender_linear(owner_coords, partner, mesh_counts)].set(second_slot.astype(jnp.int32))
        rows_out.append(jnp.stack([first_row, second_row]))
    return jnp.stack(rows_out).astype(jnp.int32)


def with_ends(entries, rng, smallest, top_value):
    longest = entries.shape.index(max(entries.shape))
    spots = []
    for shift in (0, 1):
        where = [jax.random.randint(jax.random.fold_in(rng, axis), (), 0, length) for axis, length in enumerate(entries.shape)]
        where[longest] = (where[longest] + shift) % entries.shape[longest]
        spots.append(tuple(where))
    return entries.at[spots[0]].set(smallest).at[spots[1]].set(top_value)


def levels(key, dims, shards, least, largest):
    loudness = 1.0
    for position, parts in shards:
        heights = jax.random.uniform(jax.random.fold_in(jax.random.fold_in(key, 6), position), (parts,), jnp.float32, least / len(shards), largest / len(shards))
        loudness = loudness * jnp.repeat(jnp.exp(heights), dims[position] // parts).reshape((-1,) + (1,) * (len(dims) - 1 - position))
    return loudness


def bell_draw(stream_key, extent, spread, reach, shards=(), held_as=jnp.bfloat16):
    loudness = levels(stream_key, extent, shards, -0.22, 0.18) if shards else 1.0
    array = jax.random.normal(stream_key, extent, jnp.float32) * spread * loudness
    return jnp.minimum(jnp.maximum(array, -reach), reach).astype(held_as)


def setup_inputs(seed: int = 0) -> dict:
    streams_of = jax.random.split(jax.random.key(seed), 5)
    orbitals = bell_draw(streams_of[0], (MX, MY, MZ, NMU, 2 * NB), 1.0, 6.0, ((0, 4), (1, 4), (2, 16)))
    kernel = bell_draw(streams_of[1], (OWNERS, 2, NMU, NMU), (25 * NMU * NMU * NB) ** -0.5, 0.00015258789, ((0, 256),))
    plan = draw_plan(jax.random.fold_in(streams_of[4], 71), 0)
    occupation = with_ends((jax.random.randint(streams_of[3], (MX, MY, MZ, NB), 0, 4) < 3).astype(jnp.int32), jax.random.fold_in(streams_of[3], 1), 0, 1)
    return dict(orbitals=orbitals, kernel=kernel, plan=plan, occupation=occupation)


def hop_shifts(turn_number, mesh_counts):
    forward = ((turn_number + 1) % mesh_counts[0], (2 * turn_number + 1) % mesh_counts[1], (3 * turn_number + 1) % mesh_counts[2])
    partner = (forward[0], forward[1], (forward[2] - mesh_counts[2] // 2) % mesh_counts[2])
    return forward, partner


def global_points(plan, turn_number, column, shift, owner_coords, mesh_counts, cell_counts):
    sender_first = (owner_coords[0] - shift[0]) % mesh_counts[0]
    sender_second = (owner_coords[1] - shift[1]) % mesh_counts[1]
    sender_third = (owner_coords[2] - shift[2]) % mesh_counts[2]
    linear = (sender_first * mesh_counts[1] + sender_second) * mesh_counts[2] + sender_third
    slot_index = plan[turn_number, column, linear]
    cell_first = slot_index // (cell_counts[1] * cell_counts[2])
    cell_second = (slot_index // cell_counts[2]) % cell_counts[1]
    cell_third = slot_index % cell_counts[2]
    return (sender_first * cell_counts[0] + cell_first, sender_second * cell_counts[1] + cell_second, sender_third * cell_counts[2] + cell_third)


def density_product(orbital, occupied):
    bands = orbital.shape[1] // 2
    weights = jnp.concatenate([occupied, occupied]).astype(orbital.dtype)
    masked = orbital * weights[None, :]
    swapped = jnp.concatenate([-orbital[:, bands:], orbital[:, :bands]], axis=1)
    density_real = jnp.dot(masked, orbital.T, preferred_element_type=jnp.float32)
    density_imag = jnp.dot(masked, swapped.T, preferred_element_type=jnp.float32)
    return density_real, density_imag


def kernel_hadamard(kernel_real, kernel_imag, density_real, density_imag, conjugate_sign):
    weight_real = kernel_real.astype(jnp.float32)
    weight_imag = kernel_imag.astype(jnp.float32) * conjugate_sign
    hadamard_real = weight_real * density_real - weight_imag * density_imag
    hadamard_imag = weight_real * density_imag + weight_imag * density_real
    return jnp.concatenate([hadamard_real, hadamard_imag], axis=1).astype(jnp.bfloat16)


def exchange_block(stacked, orbital):
    bands = orbital.shape[1] // 2
    real_part = orbital[:, :bands]
    imag_part = orbital[:, bands:]
    blocked = jnp.concatenate([orbital, jnp.concatenate([-imag_part, real_part], axis=1)], axis=0)
    mixture = jnp.dot(stacked, blocked, preferred_element_type=jnp.float32).astype(jnp.bfloat16)
    gram_matrix = lax.dot_general(orbital, mixture, (((0,), (0,)), ((), ())), preferred_element_type=jnp.float32)
    result_real = -(gram_matrix[:bands, :bands] + gram_matrix[bands:, bands:])
    result_imag = -(gram_matrix[:bands, bands:] - gram_matrix[bands:, :bands])
    return jnp.concatenate([result_real, result_imag], axis=1)


def pair_blocks(kernel_real, kernel_imag, orbital_first, occupied_first, orbital_second, occupied_second):
    second_real, second_imag = density_product(orbital_second, occupied_second)
    first_block = exchange_block(kernel_hadamard(kernel_real, kernel_imag, second_real, second_imag, 1.0), orbital_first)
    first_real, first_imag = density_product(orbital_first, occupied_first)
    second_block = exchange_block(kernel_hadamard(kernel_real, kernel_imag, first_real, first_imag, -1.0), orbital_second)
    return first_block, second_block


def reference(orbitals, kernel, plan, occupation):
    mesh_counts = (N_KX, N_KY, N_KZ)
    cell_counts = (CX, CY, CZ)
    owner_total = N_KX * N_KY * N_KZ
    extent_second = CY * N_KY
    extent_third = CZ * N_KZ
    point_total = CX * N_KX * extent_second * extent_third
    flat_orbitals = orbitals.reshape(point_total, NMU, 2 * NB)
    flat_occupied = occupation.reshape(point_total, NB)
    owners = jnp.arange(owner_total, dtype=jnp.int32)
    owner_coords = (owners // (N_KY * N_KZ), (owners // N_KZ) % N_KY, owners % N_KZ)
    totals = jnp.zeros((point_total, NB, 2 * NB), jnp.float32)
    for turn_number in range(ROUNDS):
        forward, partner = hop_shifts(turn_number, mesh_counts)
        first_point = global_points(plan, turn_number, 0, forward, owner_coords, mesh_counts, cell_counts)
        second_point = global_points(plan, turn_number, 1, partner, owner_coords, mesh_counts, cell_counts)
        first_linear = ((first_point[0] * extent_second + first_point[1]) * extent_third + first_point[2]).astype(jnp.int32)
        second_linear = ((second_point[0] * extent_second + second_point[1]) * extent_third + second_point[2]).astype(jnp.int32)

        def one_owner(inputs):
            owner, first_index, second_index = inputs
            local_kernel = kernel[owner]
            return pair_blocks(local_kernel[0], local_kernel[1], flat_orbitals[first_index], flat_occupied[first_index], flat_orbitals[second_index], flat_occupied[second_index])

        first_blocks, second_blocks = lax.map(one_owner, (owners, first_linear, second_linear))
        totals = totals.at[first_linear].add(first_blocks)
        totals = totals.at[second_linear].add(second_blocks)
    return totals.reshape(CX * N_KX, extent_second, extent_third, NB, 2 * NB)
```

```python
import functools

import jax
import jax.numpy as jnp
from jax import lax
from jax.experimental import pallas as pl
from jax.experimental.pallas import tpu as pltpu
from jax.sharding import PartitionSpec as P

MESH = pl.DeviceIdType.MESH
AXES = ("kx", "ky", "kz")
NT = (((1,), (1,)), ((), ()))
TN = (((0,), (0,)), ((), ()))
F32 = jnp.float32
BF16 = jnp.bfloat16
CHUNK = 256


def hop_shifts(turn, counts):
    forward = (
        (turn + 1) % counts[0],
        (2 * turn + 1) % counts[1],
        (3 * turn + 1) % counts[2],
    )
    partner = (forward[0], forward[1], (forward[2] - counts[2] // 2) % counts[2])
    return forward, partner


def exchange_kernel(counts, cells, shifts, orbitals, weights, plan, occupation, out, *scratch):
    (local, weight, occupied, sending, orbital, turned, masked, hadamard, first_sum, second_sum,
     block, returned, local_sem, weight_sem, occupied_sem, send_sem, recv_sem, back_send_sem, back_recv_sem) = scratch
    places = tuple(lax.axis_index(axis) for axis in AXES)
    points, nmu, width = orbitals.shape
    bands = width // 2
    chunks = nmu // CHUNK
    messages = len(shifts)
    turns = messages // 2

    def moved(shift, sign):
        return tuple(lax.rem(p + (sign * s) % n, n) for p, s, n in zip(places, shift, counts))

    def linear(place):
        return (place[0] * counts[1] + place[1]) * counts[2] + place[2]

    def slot_of(message, place):
        return plan[message // 2, message % 2, linear(place)]

    def rows(c):
        return pl.ds(pl.multiple_of(c * CHUNK, CHUNK), CHUNK)

    targets = [moved(shift, 1) for shift in shifts]
    sources = [moved(shift, -1) for shift in shifts]

    def orbital_copy(m, c):
        return pltpu.make_async_remote_copy(
            src_ref=sending.at[m, rows(c)],
            dst_ref=orbital.at[m, rows(c)],
            send_sem=send_sem.at[m, c],
            recv_sem=recv_sem.at[m, c],
            device_id=targets[m],
            device_id_type=MESH,
        )

    def block_copy(m):
        return pltpu.make_async_remote_copy(
            src_ref=block.at[m],
            dst_ref=returned.at[m],
            send_sem=back_send_sem.at[m],
            recv_sem=back_recv_sem.at[m],
            device_id=sources[m],
            device_id_type=MESH,
        )

    partners = {}
    for shift in shifts:
        for sign in (1, -1):
            partners[tuple((sign * s) % n for s, n in zip(shift, counts))] = moved(shift, sign)
    barrier = pltpu.get_barrier_semaphore()
    for partner in partners.values():
        pl.semaphore_signal(barrier, inc=1, device_id=partner, device_id_type=MESH)

    local_copy = pltpu.make_async_copy(orbitals, local, local_sem)
    local_copy.start()
    weight_copy = pltpu.make_async_copy(weights, weight, weight_sem)
    occupied_copies = []
    for m in range(messages):
        x, y, z = sources[m]
        occupied_copies.append(
            pltpu.make_async_copy(
                occupation.at[
                    pl.ds(x * cells[0], cells[0]),
                    pl.ds(y * cells[1], cells[1]),
                    pl.ds(pl.multiple_of(z // 8 * 8, 8), 8),
                ],
                occupied.at[m],
                occupied_sem.at[m],
            )
        )
    for copy in occupied_copies:
        copy.start()
    own_slots = [slot_of(m, places) for m in range(messages)]
    first_sum[...] = jnp.zeros_like(first_sum)
    second_sum[...] = jnp.zeros_like(second_sum)
    local_copy.wait()
    weight_copy.start()
    for m in range(0, messages, 2):
        sending[m] = local[own_slots[m]]
    pl.semaphore_wait(barrier, len(partners))
    for c in range(chunks):
        for m in range(0, messages, 2):
            orbital_copy(m, c).start()
    for m in range(1, messages, 2):
        sending[m] = local[own_slots[m]]
    for c in range(chunks):
        for m in range(1, messages, 2):
            orbital_copy(m, c).start()

    masks = []
    for copy in occupied_copies:
        copy.wait()
    for m in range(messages):
        slot = slot_of(m, sources[m])
        row = occupied[
            m, lax.div(slot, cells[1]), lax.rem(slot, cells[1]), pl.ds(lax.rem(sources[m][2], 8), 1)
        ].astype(F32)
        masks.append(jnp.concatenate([row, row], axis=1).astype(BF16))
    weight_copy.wait()

    def prepare(m, c):
        orbital_copy(m, c).wait_recv()
        part = orbital[m, rows(c)]
        turned[m, rows(c)] = jnp.concatenate([-part[:, bands:], part[:, :bands]], axis=1)
        masked[m, rows(c)] = part * masks[m]

    def stacked(m, j):
        return jnp.concatenate([orbital[m, rows(j)], turned[m, rows(j)]], axis=0)

    def product(m, i, j, sign):
        density = lax.dot_general(
            masked[m, rows(i)], stacked(m, j), NT, preferred_element_type=F32
        )
        real, imag = density[:, :CHUNK], density[:, CHUNK:]
        wr = weight[0, rows(i), rows(j)].astype(F32)
        wi = weight[1, rows(i), rows(j)].astype(F32) * sign
        return jnp.concatenate(
            [(wr * real - wi * imag).astype(BF16), (wr * imag + wi * real).astype(BF16)], axis=1
        )

    def first_step(turn, i, j):
        hadamard[turn, j, rows(i)] = product(2 * turn, i, j, -1.0)

    def second_step(turn, i, j):
        first_sum[turn, rows(i)] += jnp.dot(
            product(2 * turn + 1, i, j, 1.0), stacked(2 * turn, j), preferred_element_type=F32
        )

    def panels(step, turn, c):
        @pl.loop(0, c)
        def _(i):
            step(turn, i, c)

        @pl.loop(0, c + 1)
        def _(j):
            step(turn, c, j)

    @pl.loop(0, chunks)
    def _(c):
        for turn in range(turns):
            prepare(2 * turn, c)
            panels(first_step, turn, c)

    @pl.loop(0, chunks)
    def _(c):
        for turn in range(turns):
            prepare(2 * turn + 1, c)
            second_sum[turn] += jnp.dot(
                hadamard[turn, c], stacked(2 * turn + 1, c), preferred_element_type=F32
            )
            panels(second_step, turn, c)

    for turn in range(turns):
        for m, total in ((2 * turn, first_sum), (2 * turn + 1, second_sum)):
            gram = lax.dot_general(
                orbital[m], total[turn].astype(BF16), TN, preferred_element_type=F32
            )
            real = -(gram[:bands, :bands] + gram[bands:, bands:])
            imag = -(gram[:bands, bands:] - gram[bands:, :bands])
            block[m] = jnp.concatenate([real, imag], axis=1)
            block_copy(m).start()

    for m in range(messages):
        block_copy(m).wait_recv()
    for s in range(points):
        total = jnp.zeros((bands, width), F32)
        for m in range(messages):
            total = total + jnp.where(own_slots[m] == s, returned[m], 0.0)
        out[s] = total
    for m in range(messages):
        for c in range(chunks):
            orbital_copy(m, c).wait_send()
        block_copy(m).wait_send()


def on_device(counts, orbitals, kernel, plan, occupation):
    cells = orbitals.shape[:3]
    points = cells[0] * cells[1] * cells[2]
    nmu, width = orbitals.shape[3:]
    turns = plan.shape[0]
    shifts = [shift for turn in range(turns) for shift in hop_shifts(turn, counts)]
    messages = len(shifts)
    chunks = nmu // CHUNK
    result = pl.pallas_call(
        functools.partial(exchange_kernel, counts, cells, shifts),
        out_shape=jax.ShapeDtypeStruct((points, width // 2, width), F32),
        in_specs=[
            pl.BlockSpec(memory_space=pl.ANY),
            pl.BlockSpec(memory_space=pl.ANY),
            pl.BlockSpec(memory_space=pltpu.SMEM),
            pl.BlockSpec(memory_space=pl.ANY),
        ],
        out_specs=pl.BlockSpec(memory_space=pltpu.VMEM),
        scratch_shapes=[
            pltpu.VMEM((points, nmu, width), BF16),
            pltpu.VMEM((2, nmu, nmu), BF16),
            pltpu.VMEM((messages, cells[0], cells[1], 8, width // 2), jnp.int32),
            pltpu.VMEM((messages, nmu, width), BF16),
            pltpu.VMEM((messages, nmu, width), BF16),
            pltpu.VMEM((messages, nmu, width), BF16),
            pltpu.VMEM((messages, nmu, width), BF16),
            pltpu.VMEM((turns, chunks, nmu, 2 * CHUNK), BF16),
            pltpu.VMEM((turns, nmu, width), F32),
            pltpu.VMEM((turns, nmu, width), F32),
            pltpu.VMEM((messages, width // 2, width), F32),
            pltpu.VMEM((messages, width // 2, width), F32),
            pltpu.SemaphoreType.DMA,
            pltpu.SemaphoreType.DMA,
            pltpu.SemaphoreType.DMA((messages,)),
            pltpu.SemaphoreType.DMA((messages, chunks)),
            pltpu.SemaphoreType.DMA((messages, chunks)),
            pltpu.SemaphoreType.DMA((messages,)),
            pltpu.SemaphoreType.DMA((messages,)),
        ],
        compiler_params=pltpu.CompilerParams(
            collective_id=0, has_side_effects=True, vmem_limit_bytes=56 * 2**20
        ),
        name="exchange",
    )(orbitals.reshape(points, nmu, width), kernel[0], plan, occupation)
    return result.reshape(*cells, width // 2, width)


def solution(mesh):
    counts = tuple(mesh.shape[axis] for axis in AXES)
    return jax.shard_map(
        functools.partial(on_device, counts),
        mesh=mesh,
        in_specs=(P(*AXES, None, None), P(AXES, None, None, None), P(), P()),
        out_specs=P(*AXES, None, None),
        check_vma=False,
    )
```

```python
import functools

import jax
import jax.numpy as jnp
from jax import lax
from jax.experimental import pallas as pl
from jax.experimental.pallas import tpu as pltpu
from jax.sharding import PartitionSpec as P

MESH = pl.DeviceIdType.MESH
AXES = ("kx", "ky", "kz")
NT = (((1,), (1,)), ((), ()))
TN = (((0,), (0,)), ((), ()))
F32 = jnp.float32
BF16 = jnp.bfloat16
CHUNK = 256


def hop_shifts(turn, counts):
    forward = (
        (turn + 1) % counts[0],
        (2 * turn + 1) % counts[1],
        (3 * turn + 1) % counts[2],
    )
    partner = (forward[0], forward[1], (forward[2] - counts[2] // 2) % counts[2])
    return forward, partner


def exchange_kernel(counts, cells, shifts, orbitals, weights, plan, occupation, out, *scratch):
    (local, weight, occupied, mask_rows, sending, orbital, turned, masked, hadamard, first_sum, second_sum,
     block, returned, local_sem, weight_sem, occupied_sem, send_sem, recv_sem, back_send_sem, back_recv_sem) = scratch
    places = tuple(lax.axis_index(axis) for axis in AXES)
    points, nmu, width = orbitals.shape
    bands = width // 2
    chunks = nmu // CHUNK
    messages = len(shifts)
    turns = messages // 2

    def moved(shift, sign):
        return tuple(lax.rem(p + (sign * s) % n, n) for p, s, n in zip(places, shift, counts))

    def linear(place):
        return (place[0] * counts[1] + place[1]) * counts[2] + place[2]

    def slot_of(message, place):
        return plan[message // 2, message % 2, linear(place)]

    def rows(c):
        return pl.ds(c * CHUNK, CHUNK)

    targets = [moved(shift, 1) for shift in shifts]
    sources = [moved(shift, -1) for shift in shifts]

    def orbital_copy(m, c):
        target = targets[m] if isinstance(m, int) else targets[0]
        return pltpu.make_async_remote_copy(
            src_ref=sending.at[m, rows(c)],
            dst_ref=orbital.at[m, rows(c)],
            send_sem=send_sem.at[m, c],
            recv_sem=recv_sem.at[m, c],
            device_id=target,
            device_id_type=MESH,
        )

    def block_copy(m):
        return pltpu.make_async_remote_copy(
            src_ref=block.at[m],
            dst_ref=returned.at[m],
            send_sem=back_send_sem.at[m],
            recv_sem=back_recv_sem.at[m],
            device_id=sources[m],
            device_id_type=MESH,
        )

    partners = {}
    for shift in shifts:
        for sign in (1, -1):
            partners[tuple((sign * s) % n for s, n in zip(shift, counts))] = moved(shift, sign)
    barrier = pltpu.get_barrier_semaphore()
    for partner in partners.values():
        pl.semaphore_signal(barrier, inc=1, device_id=partner, device_id_type=MESH)

    local_copy = pltpu.make_async_copy(orbitals, local, local_sem)
    local_copy.start()
    weight_copy = pltpu.make_async_copy(weights, weight, weight_sem)
    occupied_copies = []
    for m in range(messages):
        x, y, z = sources[m]
        occupied_copies.append(
            pltpu.make_async_copy(
                occupation.at[
                    pl.ds(x * cells[0], cells[0]),
                    pl.ds(y * cells[1], cells[1]),
                    pl.ds(pl.multiple_of(z // 8 * 8, 8), 8),
                ],
                occupied.at[m],
                occupied_sem.at[m],
            )
        )
    for copy in occupied_copies:
        copy.start()
    own_slots = [slot_of(m, places) for m in range(messages)]
    local_copy.wait()
    weight_copy.start()
    for m in range(0, messages, 2):
        sending[m] = local[own_slots[m]]
    pl.semaphore_wait(barrier, len(partners))
    for c in range(chunks):
        for m in range(0, messages, 2):
            orbital_copy(m, c).start()
    for m in range(1, messages, 2):
        sending[m] = local[own_slots[m]]
    for c in range(chunks):
        for m in range(1, messages, 2):
            orbital_copy(m, c).start()

    for copy in occupied_copies:
        copy.wait()
    for m in range(messages):
        slot = slot_of(m, sources[m])
        row = occupied[
            m, lax.div(slot, cells[1]), lax.rem(slot, cells[1]), pl.ds(lax.rem(sources[m][2], 8), 1)
        ].astype(F32)
        mask_rows[m] = jnp.concatenate([row, row], axis=1)
    weight_copy.wait()

    def prepare(m, c):
        orbital_copy(m, c).wait_recv()
        part = orbital[m, rows(c)]
        turned[m, rows(c)] = jnp.concatenate([-part[:, bands:], part[:, :bands]], axis=1)
        masked[m, rows(c)] = part * mask_rows[m].astype(BF16)

    def stacked(m, low, high):
        return jnp.concatenate([orbital[m, low:high], turned[m, low:high]], axis=0)

    def product(m, top, bottom, low, high, sign):
        density = lax.dot_general(
            masked[m, top:bottom], stacked(m, low, high), NT, preferred_element_type=F32
        )
        span = high - low
        real, imag = density[:, :span], density[:, span:]
        wr = weight[0, top:bottom, low:high].astype(F32)
        wi = weight[1, top:bottom, low:high].astype(F32) * sign
        return (wr * real - wi * imag).astype(BF16), (wr * imag + wi * real).astype(BF16)

    for c in range(chunks):
        low, high = c * CHUNK, (c + 1) * CHUNK

        @pl.loop(0, turns)
        def _(turn):
            m = 2 * turn
            prepare(m, c)
            real, imag = product(m, 0, high, low, high, -1.0)
            hadamard[turn, c, :high, :CHUNK] = real
            hadamard[turn, c, :high, CHUNK:] = imag
            if c:
                real, imag = product(m, low, high, 0, low, -1.0)
                for j in range(c):
                    part = slice(j * CHUNK, (j + 1) * CHUNK)
                    hadamard[turn, j, low:high, :CHUNK] = real[:, part]
                    hadamard[turn, j, low:high, CHUNK:] = imag[:, part]

    for c in range(chunks):
        low, high = c * CHUNK, (c + 1) * CHUNK

        @pl.loop(0, turns)
        def _(turn):
            k, m = 2 * turn, 2 * turn + 1
            prepare(m, c)
            mixed = jnp.dot(hadamard[turn, c], stacked(m, low, high), preferred_element_type=F32)
            second_sum[turn] = mixed if c == 0 else second_sum[turn] + mixed
            real, imag = product(m, 0, high, low, high, 1.0)
            mixed = jnp.dot(
                jnp.concatenate([real, imag], axis=1), stacked(k, low, high), preferred_element_type=F32
            )
            if c:
                first_sum[turn, :low] += mixed[:low]
                real, imag = product(m, low, high, 0, low, 1.0)
                first_sum[turn, low:high] = mixed[low:] + jnp.dot(
                    jnp.concatenate([real, imag], axis=1), stacked(k, 0, low), preferred_element_type=F32
                )
            else:
                first_sum[turn, :high] = mixed

    for turn in range(turns):
        for m, total in ((2 * turn, first_sum), (2 * turn + 1, second_sum)):
            gram = lax.dot_general(
                orbital[m], total[turn].astype(BF16), TN, preferred_element_type=F32
            )
            real = -(gram[:bands, :bands] + gram[bands:, bands:])
            imag = -(gram[:bands, bands:] - gram[bands:, :bands])
            block[m] = jnp.concatenate([real, imag], axis=1)
            block_copy(m).start()

    for m in range(messages):
        block_copy(m).wait_recv()
    for s in range(points):
        total = jnp.zeros((bands, width), F32)
        for m in range(messages):
            total = total + jnp.where(own_slots[m] == s, returned[m], 0.0)
        out[s] = total
    for m in range(messages):
        for c in range(chunks):
            orbital_copy(m, c).wait_send()
        block_copy(m).wait_send()


def on_device(counts, orbitals, kernel, plan, occupation):
    cells = orbitals.shape[:3]
    points = cells[0] * cells[1] * cells[2]
    nmu, width = orbitals.shape[3:]
    turns = plan.shape[0]
    shifts = [shift for turn in range(turns) for shift in hop_shifts(turn, counts)]
    messages = len(shifts)
    chunks = nmu // CHUNK
    result = pl.pallas_call(
        functools.partial(exchange_kernel, counts, cells, shifts),
        out_shape=jax.ShapeDtypeStruct((points, width // 2, width), F32),
        in_specs=[
            pl.BlockSpec(memory_space=pl.ANY),
            pl.BlockSpec(memory_space=pl.ANY),
            pl.BlockSpec(memory_space=pltpu.SMEM),
            pl.BlockSpec(memory_space=pl.ANY),
        ],
        out_specs=pl.BlockSpec(memory_space=pltpu.VMEM),
        scratch_shapes=[
            pltpu.VMEM((points, nmu, width), BF16),
            pltpu.VMEM((2, nmu, nmu), BF16),
            pltpu.VMEM((messages, cells[0], cells[1], 8, width // 2), jnp.int32),
            pltpu.VMEM((messages, 1, width), F32),
            pltpu.VMEM((messages, nmu, width), BF16),
            pltpu.VMEM((messages, nmu, width), BF16),
            pltpu.VMEM((messages, nmu, width), BF16),
            pltpu.VMEM((messages, nmu, width), BF16),
            pltpu.VMEM((turns, chunks, nmu, 2 * CHUNK), BF16),
            pltpu.VMEM((turns, nmu, width), F32),
            pltpu.VMEM((turns, nmu, width), F32),
            pltpu.VMEM((messages, width // 2, width), F32),
            pltpu.VMEM((messages, width // 2, width), F32),
            pltpu.SemaphoreType.DMA,
            pltpu.SemaphoreType.DMA,
            pltpu.SemaphoreType.DMA((messages,)),
            pltpu.SemaphoreType.DMA((messages, chunks)),
            pltpu.SemaphoreType.DMA((messages, chunks)),
            pltpu.SemaphoreType.DMA((messages,)),
            pltpu.SemaphoreType.DMA((messages,)),
        ],
        compiler_params=pltpu.CompilerParams(
            collective_id=0, has_side_effects=True, vmem_limit_bytes=56 * 2**20
        ),
        name="exchange",
    )(orbitals.reshape(points, nmu, width), kernel[0], plan, occupation)
    return result.reshape(*cells, width // 2, width)


def solution(mesh):
    counts = tuple(mesh.shape[axis] for axis in AXES)
    return jax.shard_map(
        functools.partial(on_device, counts),
        mesh=mesh,
        in_specs=(P(*AXES, None, None), P(AXES, None, None, None), P(), P()),
        out_specs=P(*AXES, None, None),
        check_vma=False,
    )
```

```python
import functools

import jax
import jax.numpy as jnp
from jax import lax
from jax.experimental import pallas as pl
from jax.experimental.pallas import tpu as pltpu
from jax.sharding import PartitionSpec as P

MESH = pl.DeviceIdType.MESH
AXES = ("kx", "ky", "kz")
NT = (((1,), (1,)), ((), ()))
F32 = jnp.float32
BF16 = jnp.bfloat16
PIECE = 128
UNITS = (256, 256, 256, 128, 128)
ORDER = (0, 3, 2, 1)


def hop_shifts(turn, counts):
    forward = (
        (turn + 1) % counts[0],
        (2 * turn + 1) % counts[1],
        (3 * turn + 1) % counts[2],
    )
    partner = (forward[0], forward[1], (forward[2] - counts[2] // 2) % counts[2])
    return forward, partner


def exchange_kernel(counts, cells, shifts, orbitals, weights, plan, occupation, out, slots, *scratch):
    pieces = orbitals.shape[1] // PIECE
    local, scratch = scratch[:pieces], scratch[pieces:]
    (weight, weight_flipped, occupied, mask_rows, sending, orbital, turned, masked, flipped, flipped_turned, sums, block,
     returned, local_sem, weight_sem, occupied_sem, send_sem, recv_sem, back_send_sem, back_recv_sem) = scratch
    places = tuple(lax.axis_index(axis) for axis in AXES)
    points, nmu, width = orbitals.shape
    bands = width // 2
    messages = len(shifts)
    turns = messages // 2

    def moved(shift, sign):
        return tuple(lax.rem(p + (sign * s) % n, n) for p, s, n in zip(places, shift, counts))

    def linear(place):
        return (place[0] * counts[1] + place[1]) * counts[2] + place[2]

    def slot_of(message, place):
        return plan[message // 2, message % 2, linear(place)]

    def rows(c):
        return pl.ds(c * PIECE, PIECE)

    targets = [moved(shift, 1) for shift in shifts]
    sources = [moved(shift, -1) for shift in shifts]

    def orbital_copy(m, c):
        target = targets[m] if isinstance(m, int) else targets[0]
        return pltpu.make_async_remote_copy(
            src_ref=sending.at[m, rows(c)],
            dst_ref=orbital.at[m, rows(c)],
            send_sem=send_sem.at[m, c],
            recv_sem=recv_sem.at[m, c],
            device_id=target,
            device_id_type=MESH,
        )

    def block_copy(m):
        return pltpu.make_async_remote_copy(
            src_ref=block.at[m],
            dst_ref=returned.at[m],
            send_sem=back_send_sem.at[m],
            recv_sem=back_recv_sem.at[m],
            device_id=sources[m],
            device_id_type=MESH,
        )

    partners = {}
    for shift in shifts:
        for sign in (1, -1):
            partners[tuple((sign * s) % n for s, n in zip(shift, counts))] = moved(shift, sign)
    barrier = pltpu.get_barrier_semaphore()
    for partner in partners.values():
        pl.semaphore_signal(barrier, inc=1, device_id=partner, device_id_type=MESH)

    local_copies = [
        pltpu.make_async_copy(orbitals.at[:, rows(c)], local[c], local_sem.at[c])
        for c in range(pieces)
    ]
    for copy in local_copies:
        copy.start()
    weight_copy = pltpu.make_async_copy(weights, weight, weight_sem)
    occupied_copies = []
    for m in range(messages):
        x, y, z = sources[m]
        occupied_copies.append(
            pltpu.make_async_copy(
                occupation.at[
                    pl.ds(x * cells[0], cells[0]),
                    pl.ds(y * cells[1], cells[1]),
                    pl.ds(pl.multiple_of(z // 8 * 8, 8), 8),
                ],
                occupied.at[m],
                occupied_sem.at[m],
            )
        )
    for copy in occupied_copies:
        copy.start()
    own_slots = [slot_of(m, places) for m in range(messages)]
    for c in range(pieces):
        local_copies[c].wait()
        for m in range(messages):
            sending[m, rows(c)] = local[c][own_slots[m]]
        if c == 0:
            pl.semaphore_wait(barrier, len(partners))
        for m in ORDER:
            orbital_copy(m, c).start()
    weight_copy.start()

    for m in range(messages):
        numbers = lax.broadcasted_iota(jnp.int32, slots.shape[1:], 0)
        slots[m] = jnp.where(numbers == own_slots[m], 1.0, 0.0)
    for copy in occupied_copies:
        copy.wait()
    for m in range(messages):
        slot = slot_of(m, sources[m])
        row = occupied[
            m, lax.div(slot, cells[1]), lax.rem(slot, cells[1]), pl.ds(lax.rem(sources[m][2], 8), 1)
        ].astype(F32)
        mask_rows[m] = jnp.concatenate([row, row], axis=1)
    weight_copy.wait()
    low = UNITS[0]
    for size in UNITS[1:]:
        for part in range(2):
            weight_flipped[part, :low, low : low + size] = weight[part, low : low + size, :low].T
        low += size

    def prepare(m, low, high):
        for c in range(low // PIECE, high // PIECE):
            orbital_copy(m, c).wait_recv()
        part = orbital[m, low:high]
        turned[m, low:high] = jnp.concatenate([-part[:, bands:], part[:, :bands]], axis=1)
        masked[m, low:high] = part * mask_rows[m].astype(BF16)
        part = part.T
        flipped[m, :, low:high] = part
        flipped_turned[m, :, low:high] = jnp.concatenate([-part[bands:], part[:bands]], axis=0)

    def stacked(m, low, high):
        return jnp.concatenate([orbital[m, low:high], turned[m, low:high]], axis=0)

    def extend(m, other, sign, low, high):
        size = high - low
        density = lax.dot_general(
            masked[m, :high], stacked(m, low, high), NT, preferred_element_type=F32
        )
        real, imag = density[:, :size], density[:, size:]
        wr = weight[0, :high, low:high].astype(F32)
        wi = weight[1, :high, low:high].astype(F32) * sign
        hadamard = jnp.concatenate(
            [(wr * real - wi * imag).astype(BF16), (wr * imag + wi * real).astype(BF16)], axis=1
        )
        column = jnp.dot(hadamard, stacked(other, low, high), preferred_element_type=F32)
        if low == 0:
            sums[other, :high] = column
            return
        sums[other, :low] += column[:low]
        real, imag = real[:low], imag[:low]
        wr = weight_flipped[0, :low, low:high].astype(F32)
        wi = weight_flipped[1, :low, low:high].astype(F32) * sign
        hadamard = jnp.concatenate(
            [(wr * real + wi * imag).astype(BF16), (wi * real - wr * imag).astype(BF16)], axis=0
        )
        before = jnp.concatenate([flipped[other, :, :low], flipped_turned[other, :, :low]], axis=1)
        row = jnp.dot(before, hadamard, preferred_element_type=F32)
        sums[other, low:high] = column[low:] + row.T

    def unit(turn, low, high):
        k, p = 2 * turn, 2 * turn + 1
        prepare(k, low, high)
        prepare(p, low, high)
        extend(p, k, 1.0, low, high)
        extend(k, p, -1.0, low, high)

    low = 0
    for size in UNITS[:-1]:
        high = low + size

        @pl.loop(0, turns)
        def _(turn):
            unit(turn, low, high)

        low = high

    for turn in reversed(range(turns)):
        unit(turn, low, nmu)
        for m in (2 * turn, 2 * turn + 1):
            gram = jnp.dot(flipped[m], sums[m].astype(BF16), preferred_element_type=F32)
            real = -(gram[:bands, :bands] + gram[bands:, bands:])
            imag = -(gram[:bands, bands:] - gram[bands:, :bands])
            block[m] = jnp.concatenate([real, imag], axis=1).astype(BF16)
            block_copy(m).start()

    for m in range(messages):
        block_copy(m).wait_recv()
        out[m] = returned[m].astype(F32)
    for m in range(messages):
        for c in range(pieces):
            orbital_copy(m, c).wait_send()
        block_copy(m).wait_send()


def on_device(counts, orbitals, kernel, plan, occupation):
    cells = orbitals.shape[:3]
    points = cells[0] * cells[1] * cells[2]
    nmu, width = orbitals.shape[3:]
    turns = plan.shape[0]
    shifts = [shift for turn in range(turns) for shift in hop_shifts(turn, counts)]
    messages = len(shifts)
    pieces = nmu // PIECE
    blocks, slots = pl.pallas_call(
        functools.partial(exchange_kernel, counts, cells, shifts),
        out_shape=(
            jax.ShapeDtypeStruct((messages, width // 2, width), F32),
            jax.ShapeDtypeStruct((messages, points, width), F32),
        ),
        in_specs=[
            pl.BlockSpec(memory_space=pl.ANY),
            pl.BlockSpec(memory_space=pl.ANY),
            pl.BlockSpec(memory_space=pltpu.SMEM),
            pl.BlockSpec(memory_space=pl.ANY),
        ],
        out_specs=(pl.BlockSpec(memory_space=pltpu.VMEM),) * 2,
        scratch_shapes=[pltpu.VMEM((points, PIECE, width), BF16)] * pieces
        + [
            pltpu.VMEM((2, nmu, nmu), BF16),
            pltpu.VMEM((2, nmu, nmu), BF16),
            pltpu.VMEM((messages, cells[0], cells[1], 8, width // 2), jnp.int32),
            pltpu.VMEM((messages, 1, width), F32),
            pltpu.VMEM((messages, nmu, width), BF16),
            pltpu.VMEM((messages, nmu, width), BF16),
            pltpu.VMEM((messages, nmu, width), BF16),
            pltpu.VMEM((messages, nmu, width), BF16),
            pltpu.VMEM((messages, width, nmu), BF16),
            pltpu.VMEM((messages, width, nmu), BF16),
            pltpu.VMEM((messages, nmu, width), F32),
            pltpu.VMEM((messages, width // 2, width), BF16),
            pltpu.VMEM((messages, width // 2, width), BF16),
            pltpu.SemaphoreType.DMA((pieces,)),
            pltpu.SemaphoreType.DMA,
            pltpu.SemaphoreType.DMA((messages,)),
            pltpu.SemaphoreType.DMA((messages, pieces)),
            pltpu.SemaphoreType.DMA((messages, pieces)),
            pltpu.SemaphoreType.DMA((messages,)),
            pltpu.SemaphoreType.DMA((messages,)),
        ],
        compiler_params=pltpu.CompilerParams(
            collective_id=0, has_side_effects=True, vmem_limit_bytes=56 * 2**20
        ),
        name="exchange",
    )(orbitals.reshape(points, nmu, width), kernel[0], plan, occupation)
    total = jnp.sum(slots[:, :, None, :] * blocks[:, None], axis=0)
    return total.reshape(*cells, width // 2, width)


def solution(mesh):
    counts = tuple(mesh.shape[axis] for axis in AXES)
    return jax.shard_map(
        functools.partial(on_device, counts),
        mesh=mesh,
        in_specs=(P(*AXES, None, None), P(AXES, None, None, None), P(), P()),
        out_specs=P(*AXES, None, None),
        check_vma=False,
    )
```

```python
import functools

import jax
import jax.numpy as jnp
from jax import lax
from jax.experimental import pallas as pl
from jax.experimental.pallas import tpu as pltpu
from jax.sharding import PartitionSpec as P

MESH = pl.DeviceIdType.MESH
AXES = ("kx", "ky", "kz")
NT = (((1,), (1,)), ((), ()))
F32 = jnp.float32
BF16 = jnp.bfloat16
PIECE = 128
UNITS = (256, 256, 128, 128, 128, 128)
ORDER = (0, 3, 2, 1)


def hop_shifts(turn, counts):
    forward = (
        (turn + 1) % counts[0],
        (2 * turn + 1) % counts[1],
        (3 * turn + 1) % counts[2],
    )
    partner = (forward[0], forward[1], (forward[2] - counts[2] // 2) % counts[2])
    return forward, partner


def exchange_kernel(counts, cells, shifts, orbitals, weights, plan_table, occupation, out, slots, *scratch):
    pieces = orbitals.shape[1] // PIECE
    local, scratch = scratch[:pieces], scratch[pieces:]
    (plan, weight, weight_flipped, occupied, mask_rows, sending, orbital, turned, masked, flipped, flipped_turned, sums, block,
     returned, plan_sem, local_sem, weight_sem, occupied_sem, send_sem, recv_sem, back_send_sem, back_recv_sem) = scratch
    places = tuple(lax.axis_index(axis) for axis in AXES)
    points, nmu, width = orbitals.shape
    bands = width // 2
    messages = len(shifts)
    turns = messages // 2

    def moved(shift, sign):
        return tuple(lax.rem(p + (sign * s) % n, n) for p, s, n in zip(places, shift, counts))

    def linear(place):
        return (place[0] * counts[1] + place[1]) * counts[2] + place[2]

    def slot_of(message, place):
        return plan[message // 2, message % 2, linear(place)]

    def rows(c):
        return pl.ds(c * PIECE, PIECE)

    targets = [moved(shift, 1) for shift in shifts]
    sources = [moved(shift, -1) for shift in shifts]

    def orbital_copy(m, c):
        target = targets[m] if isinstance(m, int) else targets[0]
        return pltpu.make_async_remote_copy(
            src_ref=sending.at[m, rows(c)],
            dst_ref=orbital.at[m, rows(c)],
            send_sem=send_sem.at[m, c],
            recv_sem=recv_sem.at[m, c],
            device_id=target,
            device_id_type=MESH,
        )

    def block_copy(m):
        return pltpu.make_async_remote_copy(
            src_ref=block.at[m],
            dst_ref=returned.at[m],
            send_sem=back_send_sem.at[m],
            recv_sem=back_recv_sem.at[m],
            device_id=sources[m],
            device_id_type=MESH,
        )

    partners = {}
    for shift in shifts:
        for sign in (1, -1):
            partners[tuple((sign * s) % n for s, n in zip(shift, counts))] = moved(shift, sign)
    barrier = pltpu.get_barrier_semaphore()
    for partner in partners.values():
        pl.semaphore_signal(barrier, inc=1, device_id=partner, device_id_type=MESH)

    plan_copy = pltpu.make_async_copy(plan_table, plan, plan_sem)
    plan_copy.start()
    local_copies = [
        pltpu.make_async_copy(orbitals.at[:, rows(c)], local[c], local_sem.at[c])
        for c in range(pieces)
    ]
    for copy in local_copies:
        copy.start()
    weight_copy = pltpu.make_async_copy(weights, weight, weight_sem)
    occupied_copies = []
    for m in range(messages):
        x, y, z = sources[m]
        occupied_copies.append(
            pltpu.make_async_copy(
                occupation.at[
                    pl.ds(x * cells[0], cells[0]),
                    pl.ds(y * cells[1], cells[1]),
                    pl.ds(pl.multiple_of(z // 8 * 8, 8), 8),
                ],
                occupied.at[m],
                occupied_sem.at[m],
            )
        )
    for copy in occupied_copies:
        copy.start()
    plan_copy.wait()
    own_slots = [slot_of(m, places) for m in range(messages)]
    for c in range(pieces):
        local_copies[c].wait()
        for m in range(messages):
            sending[m, rows(c)] = local[c][own_slots[m]]
        if c == 0:
            pl.semaphore_wait(barrier, len(partners))
        for m in ORDER:
            orbital_copy(m, c).start()
    weight_copy.start()

    for m in range(messages):
        numbers = lax.broadcasted_iota(jnp.int32, slots.shape[1:], 0)
        slots[m] = jnp.where(numbers == own_slots[m], 1.0, 0.0)
    for copy in occupied_copies:
        copy.wait()
    for m in range(messages):
        slot = slot_of(m, sources[m])
        row = occupied[
            m, lax.div(slot, cells[1]), lax.rem(slot, cells[1]), pl.ds(lax.rem(sources[m][2], 8), 1)
        ].astype(F32)
        mask_rows[m] = jnp.concatenate([row, row], axis=1)
    weight_copy.wait()
    low = UNITS[0]
    for size in UNITS[1:]:
        for part in range(2):
            weight_flipped[part, :low, low : low + size] = weight[part, low : low + size, :low].T
        low += size

    def prepare(m, low, high):
        for c in range(low // PIECE, high // PIECE):
            orbital_copy(m, c).wait_recv()
        part = orbital[m, low:high]
        turned[m, low:high] = jnp.concatenate([-part[:, bands:], part[:, :bands]], axis=1)
        masked[m, low:high] = part * mask_rows[m].astype(BF16)
        part = part.T
        flipped[m, :, low:high] = part
        flipped_turned[m, :, low:high] = jnp.concatenate([-part[bands:], part[:bands]], axis=0)

    def stacked(m, low, high):
        return jnp.concatenate([orbital[m, low:high], turned[m, low:high]], axis=0)

    def extend(m, other, sign, low, high):
        size = high - low
        density = lax.dot_general(
            masked[m, :high], stacked(m, low, high), NT, preferred_element_type=F32
        )
        real, imag = density[:, :size], density[:, size:]
        wr = weight[0, :high, low:high].astype(F32)
        wi = weight[1, :high, low:high].astype(F32) * sign
        hadamard = jnp.concatenate(
            [(wr * real - wi * imag).astype(BF16), (wr * imag + wi * real).astype(BF16)], axis=1
        )
        column = jnp.dot(hadamard, stacked(other, low, high), preferred_element_type=F32)
        if low == 0:
            sums[other, :high] = column
            return
        sums[other, :low] += column[:low]
        real, imag = real[:low], imag[:low]
        wr = weight_flipped[0, :low, low:high].astype(F32)
        wi = weight_flipped[1, :low, low:high].astype(F32) * sign
        hadamard = jnp.concatenate(
            [(wr * real + wi * imag).astype(BF16), (wi * real - wr * imag).astype(BF16)], axis=0
        )
        before = jnp.concatenate([flipped[other, :, :low], flipped_turned[other, :, :low]], axis=1)
        row = jnp.dot(before, hadamard, preferred_element_type=F32)
        sums[other, low:high] = column[low:] + row.T

    def unit(turn, low, high):
        k, p = 2 * turn, 2 * turn + 1
        prepare(k, low, high)
        prepare(p, low, high)
        extend(p, k, 1.0, low, high)
        extend(k, p, -1.0, low, high)

    low = 0
    for size in UNITS[:-1]:
        high = low + size

        @pl.loop(0, turns)
        def _(turn):
            unit(turn, low, high)

        low = high

    for turn in reversed(range(turns)):
        unit(turn, low, nmu)
        for m in (2 * turn, 2 * turn + 1):
            gram = jnp.dot(flipped[m], sums[m].astype(BF16), preferred_element_type=F32)
            real = -(gram[:bands, :bands] + gram[bands:, bands:])
            imag = -(gram[:bands, bands:] - gram[bands:, :bands])
            block[m] = jnp.concatenate([real, imag], axis=1).astype(BF16)
            block_copy(m).start()

    for m in range(messages):
        block_copy(m).wait_recv()
        out[m] = returned[m].astype(F32)
    for m in range(messages):
        for c in range(pieces):
            orbital_copy(m, c).wait_send()
        block_copy(m).wait_send()


def on_device(counts, orbitals, kernel, plan, occupation):
    cells = orbitals.shape[:3]
    points = cells[0] * cells[1] * cells[2]
    nmu, width = orbitals.shape[3:]
    turns = plan.shape[0]
    shifts = [shift for turn in range(turns) for shift in hop_shifts(turn, counts)]
    messages = len(shifts)
    pieces = nmu // PIECE
    blocks, slots = pl.pallas_call(
        functools.partial(exchange_kernel, counts, cells, shifts),
        out_shape=(
            jax.ShapeDtypeStruct((messages, width // 2, width), F32),
            jax.ShapeDtypeStruct((messages, points, width), F32),
        ),
        in_specs=[
            pl.BlockSpec(memory_space=pl.ANY),
            pl.BlockSpec(memory_space=pl.ANY),
            pl.BlockSpec(memory_space=pl.ANY),
            pl.BlockSpec(memory_space=pl.ANY),
        ],
        out_specs=(pl.BlockSpec(memory_space=pltpu.VMEM),) * 2,
        scratch_shapes=[pltpu.VMEM((points, PIECE, width), BF16)] * pieces
        + [
            pltpu.SMEM(plan.shape, jnp.int32),
            pltpu.VMEM((2, nmu, nmu), BF16),
            pltpu.VMEM((2, nmu, nmu), BF16),
            pltpu.VMEM((messages, cells[0], cells[1], 8, width // 2), jnp.int32),
            pltpu.VMEM((messages, 1, width), F32),
            pltpu.VMEM((messages, nmu, width), BF16),
            pltpu.VMEM((messages, nmu, width), BF16),
            pltpu.VMEM((messages, nmu, width), BF16),
            pltpu.VMEM((messages, nmu, width), BF16),
            pltpu.VMEM((messages, width, nmu), BF16),
            pltpu.VMEM((messages, width, nmu), BF16),
            pltpu.VMEM((messages, nmu, width), F32),
            pltpu.VMEM((messages, width // 2, width), BF16),
            pltpu.VMEM((messages, width // 2, width), BF16),
            pltpu.SemaphoreType.DMA,
            pltpu.SemaphoreType.DMA((pieces,)),
            pltpu.SemaphoreType.DMA,
            pltpu.SemaphoreType.DMA((messages,)),
            pltpu.SemaphoreType.DMA((messages, pieces)),
            pltpu.SemaphoreType.DMA((messages, pieces)),
            pltpu.SemaphoreType.DMA((messages,)),
            pltpu.SemaphoreType.DMA((messages,)),
        ],
        compiler_params=pltpu.CompilerParams(
            collective_id=0, has_side_effects=True, vmem_limit_bytes=54000 * 2**10
        ),
        name="exchange",
    )(orbitals.reshape(points, nmu, width), kernel[0], plan, occupation)
    total = jnp.sum(slots[:, :, None, :] * blocks[:, None], axis=0)
    return total.reshape(*cells, width // 2, width)


def solution(mesh):
    counts = tuple(mesh.shape[axis] for axis in AXES)
    return jax.shard_map(
        functools.partial(on_device, counts),
        mesh=mesh,
        in_specs=(P(*AXES, None, None), P(AXES, None, None, None), P(), P()),
        out_specs=P(*AXES, None, None),
        check_vma=False,
    )
```

```python
import functools

import jax
import jax.numpy as jnp
from jax import lax
from jax.experimental import pallas as pl
from jax.experimental.pallas import tpu as pltpu
from jax.sharding import PartitionSpec as P

MESH = pl.DeviceIdType.MESH
AXES = ("kx", "ky", "kz")
NT = (((1,), (1,)), ((), ()))
F32 = jnp.float32
BF16 = jnp.bfloat16
PIECE = 128
UNITS = (256, 256, 128, 128, 128, 128)
ORDER = (0, 3, 2, 1)


def hop_shifts(turn, counts):
    forward = (
        (turn + 1) % counts[0],
        (2 * turn + 1) % counts[1],
        (3 * turn + 1) % counts[2],
    )
    partner = (forward[0], forward[1], (forward[2] - counts[2] // 2) % counts[2])
    return forward, partner


def exchange_kernel(counts, cells, shifts, orbitals, weights, plan_table, occupation, out, slots, *scratch):
    pieces = orbitals.shape[1] // PIECE
    local, scratch = scratch[:pieces], scratch[pieces:]
    (plan, weight, weight_flipped, occupied, mask_rows, sending, orbital, turned, masked, flipped, flipped_turned, sums, block,
     returned, plan_sem, local_sem, weight_sem, occupied_sem, send_sem, recv_sem, back_send_sem, back_recv_sem) = scratch
    places = tuple(lax.axis_index(axis) for axis in AXES)
    points, nmu, width = orbitals.shape
    bands = width // 2
    messages = len(shifts)
    turns = messages // 2

    def moved(shift, sign):
        return tuple(lax.rem(p + (sign * s) % n, n) for p, s, n in zip(places, shift, counts))

    def linear(place):
        return (place[0] * counts[1] + place[1]) * counts[2] + place[2]

    def slot_of(message, place):
        return plan[message // 2, message % 2, linear(place)]

    def rows(c):
        return pl.ds(c * PIECE, PIECE)

    targets = [moved(shift, 1) for shift in shifts]
    sources = [moved(shift, -1) for shift in shifts]

    def orbital_copy(m, c):
        target = targets[m] if isinstance(m, int) else targets[0]
        return pltpu.make_async_remote_copy(
            src_ref=sending.at[m, rows(c)],
            dst_ref=orbital.at[m, rows(c)],
            send_sem=send_sem.at[m, c],
            recv_sem=recv_sem.at[m, c],
            device_id=target,
            device_id_type=MESH,
        )

    def block_copy(m):
        return pltpu.make_async_remote_copy(
            src_ref=block.at[m],
            dst_ref=returned.at[m],
            send_sem=back_send_sem.at[m],
            recv_sem=back_recv_sem.at[m],
            device_id=sources[m],
            device_id_type=MESH,
        )

    partners = {}
    for shift in shifts:
        for sign in (1, -1):
            partners[tuple((sign * s) % n for s, n in zip(shift, counts))] = moved(shift, sign)
    barrier = pltpu.get_barrier_semaphore()
    for partner in partners.values():
        pl.semaphore_signal(barrier, inc=1, device_id=partner, device_id_type=MESH)

    plan_copy = pltpu.make_async_copy(plan_table, plan, plan_sem)
    plan_copy.start()
    local_copies = [
        pltpu.make_async_copy(orbitals.at[:, rows(c)], local[c], local_sem.at[c])
        for c in range(pieces)
    ]
    for copy in local_copies:
        copy.start()
    weight_copy = pltpu.make_async_copy(weights, weight, weight_sem)
    occupied_copies = []
    for m in range(messages):
        x, y, z = sources[m]
        occupied_copies.append(
            pltpu.make_async_copy(
                occupation.at[
                    pl.ds(x * cells[0], cells[0]),
                    pl.ds(y * cells[1], cells[1]),
                    pl.ds(pl.multiple_of(z // 8 * 8, 8), 8),
                ],
                occupied.at[m],
                occupied_sem.at[m],
            )
        )
    for copy in occupied_copies:
        copy.start()
    plan_copy.wait()
    own_slots = [slot_of(m, places) for m in range(messages)]
    for c in range(pieces):
        local_copies[c].wait()
        for m in range(messages):
            sending[m, rows(c)] = local[c][own_slots[m]]
        if c == 0:
            pl.semaphore_wait(barrier, len(partners))
        for m in ORDER:
            orbital_copy(m, c).start()
    weight_copy.start()

    for m in range(messages):
        numbers = lax.broadcasted_iota(jnp.int32, slots.shape[1:], 0)
        slots[m] = jnp.where(numbers == own_slots[m], 1.0, 0.0)
    for copy in occupied_copies:
        copy.wait()
    for m in range(messages):
        slot = slot_of(m, sources[m])
        row = occupied[
            m, lax.div(slot, cells[1]), lax.rem(slot, cells[1]), pl.ds(lax.rem(sources[m][2], 8), 1)
        ].astype(F32)
        mask_rows[m] = jnp.concatenate([row, row], axis=1)
    weight_copy.wait()
    low = UNITS[0]
    for size in UNITS[1:]:
        for part in range(2):
            weight_flipped[part, :low, low : low + size] = weight[part, low : low + size, :low].T
        low += size

    def prepare(m, low, high):
        for c in range(low // PIECE, high // PIECE):
            orbital_copy(m, c).wait_recv()
        part = orbital[m, low:high]
        turned[m, low:high] = jnp.concatenate([-part[:, bands:], part[:, :bands]], axis=1)
        masked[m, low:high] = part * mask_rows[m].astype(BF16)
        part = part.T
        flipped[m, :, low:high] = part
        flipped_turned[m, :, low:high] = jnp.concatenate([-part[bands:], part[:bands]], axis=0)

    def stacked(m, low, high):
        return jnp.concatenate([orbital[m, low:high], turned[m, low:high]], axis=0)

    def columns(m, low, high):
        return lax.dot_general(
            masked[m, :high], stacked(m, low, high), NT, preferred_element_type=F32
        )

    def extend(density, other, sign, low, high):
        size = high - low
        real, imag = density[:, :size], density[:, size:]
        wr = weight[0, :high, low:high].astype(F32)
        wi = weight[1, :high, low:high].astype(F32) * sign
        hadamard = jnp.concatenate(
            [(wr * real - wi * imag).astype(BF16), (wr * imag + wi * real).astype(BF16)], axis=1
        )
        column = jnp.dot(hadamard, stacked(other, low, high), preferred_element_type=F32)
        if low == 0:
            sums[other, :high] = column
            return
        sums[other, :low] += column[:low]
        real, imag = real[:low], imag[:low]
        wr = weight_flipped[0, :low, low:high].astype(F32)
        wi = weight_flipped[1, :low, low:high].astype(F32) * sign
        hadamard = jnp.concatenate(
            [(wr * real + wi * imag).astype(BF16), (wi * real - wr * imag).astype(BF16)], axis=0
        )
        before = jnp.concatenate([flipped[other, :, :low], flipped_turned[other, :, :low]], axis=1)
        row = jnp.dot(before, hadamard, preferred_element_type=F32)
        sums[other, low:high] = column[low:] + row.T

    def unit(turn, low, high):
        k, p = 2 * turn, 2 * turn + 1
        prepare(k, low, high)
        prepare(p, low, high)
        ofp, ofk = columns(p, low, high), columns(k, low, high)
        extend(ofp, k, 1.0, low, high)
        extend(ofk, p, -1.0, low, high)

    low = 0
    for size in UNITS[:-1]:
        high = low + size

        @pl.loop(0, turns)
        def _(turn):
            unit(turn, low, high)

        low = high

    for turn in reversed(range(turns)):
        unit(turn, low, nmu)
        for m in (2 * turn, 2 * turn + 1):
            gram = jnp.dot(flipped[m], sums[m].astype(BF16), preferred_element_type=F32)
            real = -(gram[:bands, :bands] + gram[bands:, bands:])
            imag = -(gram[:bands, bands:] - gram[bands:, :bands])
            block[m] = jnp.concatenate([real, imag], axis=1).astype(BF16)
            block_copy(m).start()

    for m in range(messages):
        for c in range(pieces):
            orbital_copy(m, c).wait_send()
    for m in range(messages):
        block_copy(m).wait_send()
    for m in reversed(range(messages)):
        block_copy(m).wait_recv()
        out[m] = returned[m].astype(F32)


def on_device(counts, orbitals, kernel, plan, occupation):
    cells = orbitals.shape[:3]
    points = cells[0] * cells[1] * cells[2]
    nmu, width = orbitals.shape[3:]
    turns = plan.shape[0]
    shifts = [shift for turn in range(turns) for shift in hop_shifts(turn, counts)]
    messages = len(shifts)
    pieces = nmu // PIECE
    blocks, slots = pl.pallas_call(
        functools.partial(exchange_kernel, counts, cells, shifts),
        out_shape=(
            jax.ShapeDtypeStruct((messages, width // 2, width), F32),
            jax.ShapeDtypeStruct((messages, points, width), F32),
        ),
        in_specs=[
            pl.BlockSpec(memory_space=pl.ANY),
            pl.BlockSpec(memory_space=pl.ANY),
            pl.BlockSpec(memory_space=pl.ANY),
            pl.BlockSpec(memory_space=pl.ANY),
        ],
        out_specs=(pl.BlockSpec(memory_space=pltpu.VMEM),) * 2,
        scratch_shapes=[pltpu.VMEM((points, PIECE, width), BF16)] * pieces
        + [
            pltpu.SMEM(plan.shape, jnp.int32),
            pltpu.VMEM((2, nmu, nmu), BF16),
            pltpu.VMEM((2, nmu, nmu), BF16),
            pltpu.VMEM((messages, cells[0], cells[1], 8, width // 2), jnp.int32),
            pltpu.VMEM((messages, 1, width), F32),
            pltpu.VMEM((messages, nmu, width), BF16),
            pltpu.VMEM((messages, nmu, width), BF16),
            pltpu.VMEM((messages, nmu, width), BF16),
            pltpu.VMEM((messages, nmu, width), BF16),
            pltpu.VMEM((messages, width, nmu), BF16),
            pltpu.VMEM((messages, width, nmu), BF16),
            pltpu.VMEM((messages, nmu, width), F32),
            pltpu.VMEM((messages, width // 2, width), BF16),
            pltpu.VMEM((messages, width // 2, width), BF16),
            pltpu.SemaphoreType.DMA,
            pltpu.SemaphoreType.DMA((pieces,)),
            pltpu.SemaphoreType.DMA,
            pltpu.SemaphoreType.DMA((messages,)),
            pltpu.SemaphoreType.DMA((messages, pieces)),
            pltpu.SemaphoreType.DMA((messages, pieces)),
            pltpu.SemaphoreType.DMA((messages,)),
            pltpu.SemaphoreType.DMA((messages,)),
        ],
        compiler_params=pltpu.CompilerParams(
            collective_id=0, has_side_effects=True, vmem_limit_bytes=54000 * 2**10
        ),
        name="exchange",
    )(orbitals.reshape(points, nmu, width), kernel[0], plan, occupation)
    total = jnp.sum(slots[:, :, None, :] * blocks[:, None], axis=0)
    return total.reshape(*cells, width // 2, width)


def solution(mesh):
    counts = tuple(mesh.shape[axis] for axis in AXES)
    return jax.shard_map(
        functools.partial(on_device, counts),
        mesh=mesh,
        in_specs=(P(*AXES, None, None), P(AXES, None, None, None), P(), P()),
        out_specs=P(*AXES, None, None),
        check_vma=False,
    )
```

```python
import functools

import jax
import jax.numpy as jnp
from jax import lax
from jax.experimental import pallas as pl
from jax.experimental.pallas import tpu as pltpu
from jax.sharding import PartitionSpec as P

MESH = pl.DeviceIdType.MESH
AXES = ("kx", "ky", "kz")
NT = (((1,), (1,)), ((), ()))
F32 = jnp.float32
BF16 = jnp.bfloat16
PIECE = 128
UNITS = (256, 256, 128, 128, 128, 128)
ORDER = (0, 3, 2, 1)


def hop_shifts(turn, counts):
    forward = (
        (turn + 1) % counts[0],
        (2 * turn + 1) % counts[1],
        (3 * turn + 1) % counts[2],
    )
    partner = (forward[0], forward[1], (forward[2] - counts[2] // 2) % counts[2])
    return forward, partner


def exchange_kernel(counts, cells, shifts, orbitals, weights, plan_table, occupation, out, slots, *scratch):
    pieces = orbitals.shape[1] // PIECE
    local, scratch = scratch[:pieces], scratch[pieces:]
    (plan, weight, weight_flipped, occupied, mask_rows, sending, orbital, turned, masked, flipped, flipped_turned, sums, block,
     returned, plan_sem, local_sem, weight_sem, occupied_sem, send_sem, recv_sem, back_send_sem, back_recv_sem) = scratch
    places = tuple(lax.axis_index(axis) for axis in AXES)
    points, nmu, width = orbitals.shape
    bands = width // 2
    messages = len(shifts)
    turns = messages // 2

    def moved(shift, sign):
        return tuple(lax.rem(p + (sign * s) % n, n) for p, s, n in zip(places, shift, counts))

    def linear(place):
        return (place[0] * counts[1] + place[1]) * counts[2] + place[2]

    def slot_of(message, place):
        return plan[message // 2, message % 2, linear(place)]

    def rows(c):
        return pl.ds(c * PIECE, PIECE)

    targets = [moved(shift, 1) for shift in shifts]
    sources = [moved(shift, -1) for shift in shifts]

    def orbital_copy(m, c):
        target = targets[m] if isinstance(m, int) else targets[0]
        return pltpu.make_async_remote_copy(
            src_ref=sending.at[m, rows(c)],
            dst_ref=orbital.at[m, rows(c)],
            send_sem=send_sem.at[m, c],
            recv_sem=recv_sem.at[m, c],
            device_id=target,
            device_id_type=MESH,
        )

    def block_copy(m, source=None):
        return pltpu.make_async_remote_copy(
            src_ref=block.at[m],
            dst_ref=returned.at[m],
            send_sem=back_send_sem.at[m],
            recv_sem=back_recv_sem.at[m],
            device_id=sources[m] if source is None else source,
            device_id_type=MESH,
        )

    partners = {}
    for shift in shifts:
        for sign in (1, -1):
            partners[tuple((sign * s) % n for s, n in zip(shift, counts))] = moved(shift, sign)
    barrier = pltpu.get_barrier_semaphore()
    for partner in partners.values():
        pl.semaphore_signal(barrier, inc=1, device_id=partner, device_id_type=MESH)

    plan_copy = pltpu.make_async_copy(plan_table, plan, plan_sem)
    plan_copy.start()
    local_copies = [
        pltpu.make_async_copy(orbitals.at[:, rows(c)], local[c], local_sem.at[c])
        for c in range(pieces)
    ]
    for copy in local_copies[:2]:
        copy.start()
    weight_copy = pltpu.make_async_copy(weights, weight, weight_sem)
    occupied_copies = []
    for m in range(messages):
        x, y, z = sources[m]
        occupied_copies.append(
            pltpu.make_async_copy(
                occupation.at[
                    pl.ds(x * cells[0], cells[0]),
                    pl.ds(y * cells[1], cells[1]),
                    pl.ds(pl.multiple_of(z // 8 * 8, 8), 8),
                ],
                occupied.at[m],
                occupied_sem.at[m],
            )
        )
    plan_copy.wait()
    own_slots = [slot_of(m, places) for m in range(messages)]
    for c in range(pieces):
        local_copies[c].wait()
        if c + 2 < pieces:
            local_copies[c + 2].start()
        for m in range(messages):
            sending[m, rows(c)] = local[c][own_slots[m]]
        if c == 0:
            pl.semaphore_wait(barrier, len(partners))
        for m in ORDER:
            orbital_copy(m, c).start()
    weight_copy.start()
    for copy in occupied_copies:
        copy.start()

    for m in range(messages):
        numbers = lax.broadcasted_iota(jnp.int32, slots.shape[1:], 0)
        slots[m] = jnp.where(numbers == own_slots[m], 1.0, 0.0)
    for copy in occupied_copies:
        copy.wait()
    for m in range(messages):
        slot = slot_of(m, sources[m])
        row = occupied[
            m, lax.div(slot, cells[1]), lax.rem(slot, cells[1]), pl.ds(lax.rem(sources[m][2], 8), 1)
        ].astype(F32)
        mask_rows[m] = jnp.concatenate([row, row], axis=1)
    weight_copy.wait()
    low = UNITS[0]
    for size in UNITS[1:]:
        for part in range(2):
            weight_flipped[part, :low, low : low + size] = weight[part, low : low + size, :low].T
        low += size

    def prepare(m, low, high):
        for c in range(low // PIECE, high // PIECE):
            orbital_copy(m, c).wait_recv()
        part = orbital[m, low:high]
        turned[m, low:high] = jnp.concatenate([-part[:, bands:], part[:, :bands]], axis=1)
        masked[m, low:high] = part * mask_rows[m].astype(BF16)
        part = part.T
        flipped[m, :, low:high] = part
        flipped_turned[m, :, low:high] = jnp.concatenate([-part[bands:], part[:bands]], axis=0)

    def stacked(m, low, high):
        return jnp.concatenate([orbital[m, low:high], turned[m, low:high]], axis=0)

    def columns(m, low, high):
        return lax.dot_general(
            masked[m, :high], stacked(m, low, high), NT, preferred_element_type=F32
        )

    def extend(density, other, sign, low, high):
        size = high - low
        real, imag = density[:, :size], density[:, size:]
        wr = weight[0, :high, low:high].astype(F32)
        wi = weight[1, :high, low:high].astype(F32) * sign
        hadamard = jnp.concatenate(
            [(wr * real - wi * imag).astype(BF16), (wr * imag + wi * real).astype(BF16)], axis=1
        )
        column = jnp.dot(hadamard, stacked(other, low, high), preferred_element_type=F32)
        if low == 0:
            sums[other, :high] = column
            return
        sums[other, :low] += column[:low]
        real, imag = real[:low], imag[:low]
        wr = weight_flipped[0, :low, low:high].astype(F32)
        wi = weight_flipped[1, :low, low:high].astype(F32) * sign
        hadamard = jnp.concatenate(
            [(wr * real + wi * imag).astype(BF16), (wi * real - wr * imag).astype(BF16)], axis=0
        )
        before = jnp.concatenate([flipped[other, :, :low], flipped_turned[other, :, :low]], axis=1)
        row = jnp.dot(before, hadamard, preferred_element_type=F32)
        sums[other, low:high] = column[low:] + row.T

    def unit(turn, low, high):
        k, p = 2 * turn, 2 * turn + 1
        prepare(k, low, high)
        prepare(p, low, high)
        ofp, ofk = columns(p, low, high), columns(k, low, high)
        extend(ofp, k, 1.0, low, high)
        extend(ofk, p, -1.0, low, high)

    low = 0
    for size in UNITS[:-1]:
        high = low + size

        @pl.loop(0, turns)
        def _(turn):
            unit(turn, low, high)

        low = high

    @pl.loop(0, turns)
    def _(step):
        turn = turns - 1 - step
        unit(turn, low, nmu)
        forward, partner = hop_shifts(turn, counts)
        for m, shift in ((2 * turn, forward), (2 * turn + 1, partner)):
            gram = jnp.dot(flipped[m], sums[m].astype(BF16), preferred_element_type=F32)
            real = -(gram[:bands, :bands] + gram[bands:, bands:])
            imag = -(gram[:bands, bands:] - gram[bands:, :bands])
            block[m] = jnp.concatenate([real, imag], axis=1).astype(BF16)
            source = tuple(lax.rem(p - h + n, n) for p, h, n in zip(places, shift, counts))
            block_copy(m, source).start()

    for m in range(messages):
        for c in range(pieces):
            orbital_copy(m, c).wait_send()
    for m in range(messages):
        block_copy(m).wait_send()
    for m in reversed(range(messages)):
        block_copy(m).wait_recv()
        out[m] = returned[m].astype(F32)


def on_device(counts, orbitals, kernel, plan, occupation):
    cells = orbitals.shape[:3]
    points = cells[0] * cells[1] * cells[2]
    nmu, width = orbitals.shape[3:]
    turns = plan.shape[0]
    shifts = [shift for turn in range(turns) for shift in hop_shifts(turn, counts)]
    messages = len(shifts)
    pieces = nmu // PIECE
    blocks, slots = pl.pallas_call(
        functools.partial(exchange_kernel, counts, cells, shifts),
        out_shape=(
            jax.ShapeDtypeStruct((messages, width // 2, width), F32),
            jax.ShapeDtypeStruct((messages, points, width), F32),
        ),
        in_specs=[
            pl.BlockSpec(memory_space=pl.ANY),
            pl.BlockSpec(memory_space=pl.ANY),
            pl.BlockSpec(memory_space=pl.ANY),
            pl.BlockSpec(memory_space=pl.ANY),
        ],
        out_specs=(pl.BlockSpec(memory_space=pltpu.VMEM),) * 2,
        scratch_shapes=[pltpu.VMEM((points, PIECE, width), BF16)] * pieces
        + [
            pltpu.SMEM(plan.shape, jnp.int32),
            pltpu.VMEM((2, nmu, nmu), BF16),
            pltpu.VMEM((2, nmu, nmu), BF16),
            pltpu.VMEM((messages, cells[0], cells[1], 8, width // 2), jnp.int32),
            pltpu.VMEM((messages, 1, width), F32),
            pltpu.VMEM((messages, nmu, width), BF16),
            pltpu.VMEM((messages, nmu, width), BF16),
            pltpu.VMEM((messages, nmu, width), BF16),
            pltpu.VMEM((messages, nmu, width), BF16),
            pltpu.VMEM((messages, width, nmu), BF16),
            pltpu.VMEM((messages, width, nmu), BF16),
            pltpu.VMEM((messages, nmu, width), F32),
            pltpu.VMEM((messages, width // 2, width), BF16),
            pltpu.VMEM((messages, width // 2, width), BF16),
            pltpu.SemaphoreType.DMA,
            pltpu.SemaphoreType.DMA((pieces,)),
            pltpu.SemaphoreType.DMA,
            pltpu.SemaphoreType.DMA((messages,)),
            pltpu.SemaphoreType.DMA((messages, pieces)),
            pltpu.SemaphoreType.DMA((messages, pieces)),
            pltpu.SemaphoreType.DMA((messages,)),
            pltpu.SemaphoreType.DMA((messages,)),
        ],
        compiler_params=pltpu.CompilerParams(
            collective_id=0, has_side_effects=True, vmem_limit_bytes=54000 * 2**10
        ),
        name="exchange",
    )(orbitals.reshape(points, nmu, width), kernel[0], plan, occupation)
    total = jnp.sum(slots[:, :, None, :] * blocks[:, None], axis=0)
    return total.reshape(*cells, width // 2, width)


def solution(mesh):
    counts = tuple(mesh.shape[axis] for axis in AXES)
    return jax.shard_map(
        functools.partial(on_device, counts),
        mesh=mesh,
        in_specs=(P(*AXES, None, None), P(AXES, None, None, None), P(), P()),
        out_specs=P(*AXES, None, None),
        check_vma=False,
    )
```
